256 devices in a mesh: rows: 64 (over y, z, core), tau: 4 (over x).
Axes of the slice: x: 4, y: 4, z: 8, core: 2. Of those that a mesh axis runs over, the one named last changes fastest.
Arguments:
- chi_grad: bfloat16 [4, 8192, 8192], P('tau', 'rows'), may hold values from -6 to 6
- green_unocc: bfloat16 [4, 8192, 8192], P('tau', 'rows'), may hold values from -6 to 6
- orbitals: bfloat16 [8192, 1536], P('rows'), may hold values from -0.0625 to 0.0625
- tau_points: float32 [4], P('tau'), may hold values from 0.1 to 2
- energy: float32 [1536], replicated, may hold values from 0.05 to 2
Outputs:
- orbital_grad: float32 [8192, 1536], P('rows', 'tau')
The draws below stay inside these ranges and needn't reach their ends.
All inputs are finite; a program needn't handle non-finite values.
Results may differ from the reference program's by a relative error of at most 0.0029.
Values may be sent and summed in bfloat16 or wider, within the bound.
A program may use at most 192 MiB of HBM per device.

```python
import math
import jax
import jax.numpy as jnp

NPTS = 8192
NOCC = 1536
TAUS = 4


def block_scale(own_key, dims, pieces, least, high):
    factor_of, own = 1.0, jax.random.fold_in(own_key, 6)
    for position, parts in pieces:
        heights = jnp.exp(jax.random.uniform(jax.random.fold_in(own, position), (parts,), jnp.float32, least / len(pieces), high / len(pieces)))
        factor_of = factor_of * jnp.repeat(heights, dims[position] // parts).reshape([-1 if axis == position else 1 for axis in range(len(dims))])
    return factor_of


def normal_values(key, dims, width, most, split=(), held_as=jnp.bfloat16):
    factor_of = block_scale(key, dims, split, -0.22, 0.18) if split else 1.0
    result = jax.random.normal(key, dims, jnp.float32) * width * factor_of
    return jnp.minimum(jnp.maximum(result, -most), most).astype(held_as)


def setup_inputs(seed: int = 0) -> dict:
    keys = jax.random.split(jax.random.key(seed), 6)
    return {
        "chi_grad": normal_values(keys[0], (TAUS, NPTS, NPTS), 1.0, 6.0, ((0, 4), (1, 64))),
        "green_unocc": normal_values(keys[1], (TAUS, NPTS, NPTS), 1.0, 6.0, ((0, 4), (1, 64))),
        "orbitals": normal_values(keys[2], (NPTS, NOCC), NPTS ** -0.5, 0.0625, ((0, 64),)),
        "tau_points": jnp.clip(0.1 + 1.9 * jax.random.uniform(keys[3], (TAUS,), jnp.float32) ** block_scale(keys[3], (TAUS,), ((0, 4),), -0.2, 0.2), 0.1, 2.0),
        "energy": jnp.clip(jnp.exp(jax.random.uniform(keys[4], (NOCC,), jnp.float32, math.log(0.05), math.log(2.0))), 0.05, 2.0),
    }


def reference(chi_grad, green_unocc, orbitals, tau_points, energy):
    orbs = orbitals.astype(jnp.float32)
    summed = jnp.zeros((NPTS, NOCC), jnp.float32)
    for index in range(TAUS):
        occ_grad = (chi_grad[index].astype(jnp.float32) * green_unocc[index].astype(jnp.float32)).astype(jnp.bfloat16)
        matrix = occ_grad.astype(jnp.float32)
        sym_prod = jnp.dot(matrix, orbs) + jnp.dot(matrix.T, orbs)
        weights = jnp.exp(-energy * tau_points[index])
        summed = summed + sym_prod * weights[None, :]
    return summed
```

```python
import functools

import jax
import jax.numpy as jnp
from jax import lax
from jax.experimental import pallas as pl
from jax.experimental.pallas import tpu as pltpu
from jax.sharding import PartitionSpec as P

MESH = pl.DeviceIdType.MESH
X, Y, Z, C = 4, 4, 8, 2
ROWS = 128
SUB = ROWS // X
NPTS = ROWS * Y * Z * C
COLS = NPTS // (X * Y)
SPAN = NPTS // Y
NOCC = 1536
NB = NOCC // X
GROUP = X * ROWS


def kernel(
    chi, green, orb, tau, energy, out,
    chi_v, green_v, sbuf, blocks, blocks_t, orb_r, orb_c, scaled_r, scaled_c, taus,
    p1, p2, p2_sib, p2_rx, p2_tx, r1, r2, f_tx, f_rx,
    load_sem, own_sem, tau_s, tau_r, or_s, or_r, oc_s, oc_r, os_s, os_r, aa_s, aa_r,
    p1_s, p1_r, sib_s, sib_r, p2_s, p2_r, f_s, f_r,
):
    x = lax.axis_index("tau")
    row = lax.axis_index("rows")
    y, q = row // (Z * C), row % (Z * C)
    z, c = q // C, q % C

    def at(dx=0, dy=0, dz=0, flip=False):
        core = 1 - c if flip else c
        return (((y + dy) % Y) * (Z * C) + ((z + dz) % Z) * C + core, (x + dx) % X)

    def remote(src, dst, s, r, dev):
        return pltpu.make_async_remote_copy(
            src_ref=src, dst_ref=dst, send_sem=s, recv_sem=r, device_id=dev, device_id_type=MESH
        )

    loads = []
    for dy in range(Y):
        cols = pl.ds(pl.multiple_of(((y + dy) % Y) * SPAN, SPAN), SPAN)
        pair = [
            pltpu.make_async_copy(chi.at[:, cols], chi_v.at[dy], load_sem.at[0, dy]),
            pltpu.make_async_copy(green.at[:, cols], green_v.at[dy], load_sem.at[1, dy]),
        ]
        for cp in pair:
            cp.start()
        loads.append(pair)
    mine = orb.at[pl.ds(pl.multiple_of(x * SUB, SUB), SUB)]
    own = [
        pltpu.make_async_copy(orb, orb_r.at[0], own_sem.at[0]),
        pltpu.make_async_copy(mine, orb_c.at[q], own_sem.at[1]),
    ]
    for cp in own:
        cp.start()

    barrier = pltpu.get_barrier_semaphore()
    for dx in range(X):
        for dy in range(Y):
            if dx or dy:
                pl.semaphore_signal(barrier, inc=1, device_id=at(dx, dy), device_id_type=MESH)
    for dz in range(1, Z):
        pl.semaphore_signal(barrier, inc=1, device_id=at(dz=dz), device_id_type=MESH)
    pl.semaphore_signal(barrier, inc=1, device_id=at(flip=True), device_id_type=MESH)
    pl.semaphore_wait(barrier, X * Y - 1 + Z - 1 + 1)

    sent = []

    def go(cp):
        cp.start()
        sent.append(cp)
        return cp

    orb_r_in = [go(remote(orb, orb_r.at[dy], or_s.at[dy], or_r.at[dy], at(dy=dy))) for dy in range(1, Y)]
    oc_in = [go(remote(mine, orb_c.at[q], oc_s.at[dz], oc_r.at[dz], at(dz=dz))) for dz in range(1, Z)]
    os_in = [go(remote(mine, orb_c.at[q], os_s.at[0], os_r.at[0], at(flip=True)))]
    taus[0] = jnp.full((8, 128), tau[0], jnp.float32)
    tau_in = [go(remote(taus.at[0], taus.at[dx], tau_s.at[dx], tau_r.at[dx], at(dx=dx))) for dx in range(1, X)]

    src = lax.broadcasted_iota(jnp.int32, (GROUP, GROUP), 0)
    dst = lax.broadcasted_iota(jnp.int32, (GROUP, GROUP), 1)
    origin = ((dst // SUB) % X) * ROWS + (dst // ROWS) * SUB + dst % SUB
    sort = jnp.where(src == origin, 1.0, 0.0).astype(jnp.bfloat16)

    aa_in = {}
    for dy in range(Y):
        for cp in loads[dy]:
            cp.wait()
        for g in range(SPAN // GROUP):
            cols = slice(g * GROUP, (g + 1) * GROUP)
            occ = (
                chi_v[dy, :, cols].astype(jnp.float32) * green_v[dy, :, cols].astype(jnp.float32)
            ).astype(jnp.bfloat16)
            packed = jnp.dot(occ, sort, preferred_element_type=jnp.float32).astype(jnp.bfloat16)
            for k in range(X):
                sbuf[dy, k, :, g * ROWS:(g + 1) * ROWS] = packed[:, k * ROWS:(k + 1) * ROWS]
        for dx in range(X):
            part = sbuf.at[dy, (x + dx) % X]
            if dx or dy:
                aa_in[dx, dy] = go(
                    remote(part, blocks.at[dx, dy], aa_s.at[dx, dy], aa_r.at[dx, dy], at(dx, dy))
                )
            else:
                keep = pltpu.make_async_copy(part, blocks.at[0, 0], own_sem.at[2])
                keep.start()

    for cp in own:
        cp.wait()
    for dz in range(1, Z):
        oc_in[dz - 1].wait_recv()
        slot = ((z - dz) % Z) * C + c
        os_in.append(go(remote(orb_c.at[slot], orb_c.at[slot], os_s.at[dz], os_r.at[dz], at(flip=True))))
    for cp in tau_in:
        cp.wait_recv()
    weights = [jnp.exp(-taus[dx][:1, :1] * energy[...]) for dx in range(X)]
    for cp in os_in:
        cp.wait_recv()
    for dx in range(X):
        for k in range(Z * C):
            scaled_c[dx, k * SUB:(k + 1) * SUB] = (orb_c[k].astype(jnp.float32) * weights[dx]).astype(jnp.bfloat16)
    for dy in range(Y):
        if dy:
            orb_r_in[dy - 1].wait_recv()
        for dx in range(X):
            scaled_r[dx * Y + dy] = (orb_r[dy].astype(jnp.float32) * weights[dx]).astype(jnp.bfloat16)

    for dy in range(Y):
        for dx in range(X):
            if dx or dy:
                aa_in[dx, dy].wait_recv()
            else:
                keep.wait()
            k = dx * Y + dy
            blocks_t[:, k * ROWS:(k + 1) * ROWS] = blocks[dx, dy].T

    for n in range(X):
        cols = slice(n * NB, (n + 1) * NB)
        rhs = scaled_r[:, :, cols].reshape(X * Y * ROWS, NB)
        acc = jnp.dot(blocks_t[...], rhs, preferred_element_type=jnp.float32)
        p2[:, :, :, cols] = acc.reshape(Z, C, SUB, NB)
    p2_sib[...] = p2[:, 1 - c].astype(jnp.bfloat16)
    sib = go(remote(p2_sib, p2_rx, sib_s, sib_r, at(flip=True)))

    p1_in = []

    def rows_part(dx):
        cols = pl.ds(pl.multiple_of(((x + dx) % X) * NB, NB), NB)
        acc = jnp.zeros((Y * ROWS, NB), jnp.float32)
        for k in range(X):
            acc += jnp.dot(
                blocks[k].reshape(Y * ROWS, COLS), scaled_c[k, :, cols], preferred_element_type=jnp.float32
            )
        p1[dx] = acc.astype(jnp.bfloat16).reshape(Y, ROWS, NB)
        for dy in range(Y):
            if dx or dy:
                p1_in.append(
                    go(remote(p1.at[dx, dy], r1.at[dx, dy], p1_s.at[dx, dy], p1_r.at[dx, dy], at(dx, -dy)))
                )

    rows_part(1)
    rows_part(2)
    sib.wait_recv()
    p2_tx[...] = (p2[:, c] + p2_rx[...].astype(jnp.float32)).astype(jnp.bfloat16)
    p2_in = [
        go(remote(p2_tx.at[(z + dz) % Z], r2.at[dz], p2_s.at[dz], p2_r.at[dz], at(dz=dz))) for dz in range(1, Z)
    ]
    rows_part(3)
    rows_part(0)

    total = p2_tx[z].astype(jnp.float32)
    for dz in range(1, Z):
        p2_in[dz - 1].wait_recv()
        total += r2[dz].astype(jnp.float32)
    for n in range(X):
        f_tx[n] = total[:, n * NB:(n + 1) * NB]
    f_in = [
        go(remote(f_tx.at[(x + dx) % X], f_rx.at[dx], f_s.at[dx], f_r.at[dx], at(dx=dx))) for dx in range(1, X)
    ]
    total = p1[0, 0].astype(jnp.float32)
    for cp in p1_in:
        cp.wait_recv()
    for dx in range(X):
        for dy in range(Y):
            if dx or dy:
                total += r1[dx, dy].astype(jnp.float32)
    out[...] = total
    out[pl.ds(pl.multiple_of(x * SUB, SUB), SUB)] += f_tx[x]
    for dx in range(1, X):
        f_in[dx - 1].wait_recv()
        out[pl.ds(pl.multiple_of(((x - dx) % X) * SUB, SUB), SUB)] += f_rx[dx]
    for cp in sent:
        cp.wait_send()


def per_device(chi_grad, green_unocc, orbitals, tau_points, energy):
    bf16, f32 = jnp.bfloat16, jnp.float32
    dma, vmem = pltpu.SemaphoreType.DMA, pltpu.VMEM
    hbm = pl.BlockSpec(memory_space=pl.ANY)
    return pl.pallas_call(
        kernel,
        out_shape=jax.ShapeDtypeStruct((ROWS, NB), f32),
        in_specs=[
            hbm, hbm, hbm,
            pl.BlockSpec(memory_space=pltpu.SMEM),
            pl.BlockSpec(memory_space=pltpu.VMEM),
        ],
        out_specs=pl.BlockSpec(memory_space=pltpu.VMEM),
        scratch_shapes=[
            vmem((Y, ROWS, SPAN), bf16), vmem((Y, ROWS, SPAN), bf16),
            vmem((Y, X, ROWS, COLS), bf16), vmem((X, Y, ROWS, COLS), bf16), vmem((COLS, X * Y * ROWS), bf16),
            vmem((Y, ROWS, NOCC), bf16), vmem((Z * C, SUB, NOCC), bf16),
            vmem((X * Y, ROWS, NOCC), bf16), vmem((X, COLS, NOCC), bf16),
            vmem((X, 8, 128), f32),
            vmem((X, Y, ROWS, NB), bf16), vmem((Z, C, SUB, NOCC), f32),
            vmem((Z, SUB, NOCC), bf16), vmem((Z, SUB, NOCC), bf16), vmem((Z, SUB, NOCC), bf16),
            vmem((X, Y, ROWS, NB), bf16), vmem((Z, SUB, NOCC), bf16),
            vmem((X, SUB, NB), f32), vmem((X, SUB, NB), f32),
            dma((2, Y)), dma((3,)), dma((X,)), dma((X,)), dma((Y,)), dma((Y,)), dma((Z,)), dma((Z,)), dma((Z,)), dma((Z,)),
            dma((X, Y)), dma((X, Y)), dma((X, Y)), dma((X, Y)), dma, dma, dma((Z,)), dma((Z,)), dma((X,)), dma((X,)),
        ],
        compiler_params=pltpu.CompilerParams(
            collective_id=1, has_side_effects=True, vmem_limit_bytes=56 * 2**20
        ),
        cost_estimate=pl.CostEstimate(flops=4 * ROWS * NPTS * NOCC, bytes_accessed=5 * 2**20, transcendentals=X * NOCC),
        name="response_backward",
    )(chi_grad[0], green_unocc[0], orbitals, tau_points, energy.reshape(1, NOCC))


def solution(mesh):
    return jax.shard_map(
        per_device,
        mesh=mesh,
        in_specs=(P("tau", "rows", None), P("tau", "rows", None), P("rows", None), P("tau"), P()),
        out_specs=P("rows", "tau"),
        check_vma=False,
    )
```

```python
import jax
import jax.numpy as jnp
from jax import lax
from jax.experimental import pallas as pl
from jax.experimental.pallas import tpu as pltpu
from jax.sharding import PartitionSpec as P

MESH = pl.DeviceIdType.MESH
BF16, F32 = jnp.bfloat16, jnp.float32
X, Y, Z, C = 4, 4, 8, 2
ROWS = 128
SUB = ROWS // X
NPTS = ROWS * Y * Z * C
COLS = NPTS // (X * Y)
SPAN = NPTS // Y
NOCC = 1536
NB = NOCC // X
GROUP = X * ROWS


def kernel(
    chi, green, orb, tau, energy, out,
    chi_v, green_v, occ_v, sbuf, blocks, blocks_t, orb_r, orb_c, taus,
    p1, r1x, p1y, r1y, p2, p2_sib, p2_rx, p2_tx, r2, f_tx, f_rx,
    load_sem, own_sem, tau_s, tau_r, or_s, or_r, oc_s, oc_r, os_s, os_r, aa_s, aa_r,
    px_s, px_r, py_s, py_r, sib_s, sib_r, p2_s, p2_r, f_s, f_r,
):
    x = lax.axis_index("tau")
    row = lax.axis_index("rows")
    y, q = row // (Z * C), row % (Z * C)
    z, c = q // C, q % C

    def at(dx=0, dy=0, dz=0, flip=False):
        core = 1 - c if flip else c
        return (((y + dy) % Y) * (Z * C) + ((z + dz) % Z) * C + core, (x + dx) % X)

    def remote(src, dst, s, r, dev):
        return pltpu.make_async_remote_copy(
            src_ref=src, dst_ref=dst, send_sem=s, recv_sem=r, device_id=dev, device_id_type=MESH
        )

    def nblock(k):
        return pl.ds(pl.multiple_of(((x + k) % X) * NB, NB), NB)

    order = (2, 1, 3, 0)
    loads = {}
    for dy in order:
        cols = pl.ds(pl.multiple_of(((y + dy) % Y) * SPAN, SPAN), SPAN)
        loads[dy] = [
            pltpu.make_async_copy(chi.at[:, cols], chi_v.at[dy], load_sem.at[0, dy]),
            pltpu.make_async_copy(green.at[:, cols], green_v.at[dy], load_sem.at[1, dy]),
        ]
        for cp in loads[dy]:
            cp.start()
    mine = orb.at[pl.ds(pl.multiple_of(x * SUB, SUB), SUB)]
    own = [pltpu.make_async_copy(mine, orb_c.at[q], own_sem.at[0])]
    for k in range(X):
        own.append(pltpu.make_async_copy(orb.at[:, nblock(k)], orb_r.at[k, 0], own_sem.at[2 + k]))
    for cp in own:
        cp.start()

    barrier = pltpu.get_barrier_semaphore()
    for dx in range(X):
        for dy in range(Y):
            if dx or dy:
                pl.semaphore_signal(barrier, inc=1, device_id=at(dx, dy), device_id_type=MESH)
    for dz in range(1, Z):
        pl.semaphore_signal(barrier, inc=1, device_id=at(dz=dz), device_id_type=MESH)
    pl.semaphore_signal(barrier, inc=1, device_id=at(flip=True), device_id_type=MESH)

    dst = lax.broadcasted_iota(jnp.int32, (8, GROUP), 1)
    origin = ((dst // SUB) % X) * ROWS + (dst // ROWS) * SUB + dst % SUB
    src = lax.broadcasted_iota(jnp.int32, (GROUP, GROUP), 0)
    sort = jnp.where(src == origin[:1], 1.0, 0.0).astype(BF16)

    def make(dy):
        for cp in loads[dy]:
            cp.wait()
        groups = SPAN // GROUP
        for g in range(groups):
            cols = slice(g * GROUP, (g + 1) * GROUP)
            occ_v[g] = (chi_v[dy, :, cols].astype(F32) * green_v[dy, :, cols].astype(F32)).astype(BF16)
        packed = jnp.dot(occ_v[...].reshape(groups * ROWS, GROUP), sort, preferred_element_type=F32).astype(BF16)
        for g in range(groups):
            for k in range(X):
                sbuf[dy, k, :, g * ROWS:(g + 1) * ROWS] = packed[g * ROWS:(g + 1) * ROWS, k * ROWS:(k + 1) * ROWS]

    sent = []

    def go(cp):
        cp.start()
        sent.append(cp)
        return cp

    aa_in = {}

    def send_blocks(dy):
        for dx in order:
            part = sbuf.at[dy, (x + dx) % X]
            if dx or dy:
                cp = remote(part, blocks.at[dx, dy], aa_s.at[dx, dy], aa_r.at[dx, dy], at(dx, dy))
                cp.start()
                aa_in[dx, dy] = cp
            else:
                keep = pltpu.make_async_copy(part, blocks.at[0, 0], own_sem.at[1])
                keep.start()
                aa_in[0, 0] = keep

    or_in = {}

    def send_orb(k):
        for dy in order[:3]:
            or_in[k, dy] = go(
                remote(orb.at[:, nblock(k)], orb_r.at[k, dy], or_s.at[k, dy], or_r.at[k, dy], at(dy=dy))
            )

    taus[0] = jnp.full((8, 128), tau[0], F32)
    make(2)
    make(1)
    pl.semaphore_wait(barrier, X * Y - 1 + Z - 1 + 1)
    send_blocks(2)
    send_blocks(1)
    oc_in = {
        dz: go(remote(mine, orb_c.at[q], oc_s.at[dz], oc_r.at[dz], at(dz=dz))) for dz in (4, 3, 5, 2, 6, 1, 7)
    }
    os_in = [go(remote(mine, orb_c.at[q], os_s.at[0], os_r.at[0], at(flip=True)))]
    tau_in = [go(remote(taus.at[0], taus.at[dx], tau_s.at[dx], tau_r.at[dx], at(dx=dx))) for dx in range(1, X)]
    make(3)
    send_blocks(3)
    make(0)
    send_blocks(0)
    send_orb(1)

    for cp in own:
        cp.wait()
    for dz in (1, 7, 2, 6, 3, 5, 4):
        oc_in[dz].wait_recv()
        slot = ((z - dz) % Z) * C + c
        os_in.append(go(remote(orb_c.at[slot], orb_c.at[slot], os_s.at[dz], os_r.at[dz], at(flip=True))))
    for cp in tau_in:
        cp.wait_recv()

    def arrive(dx, dy):
        if dx or dy:
            aa_in[dx, dy].wait_recv()
        else:
            aa_in[0, 0].wait()
        blocks_t[dx, :, dy * ROWS:(dy + 1) * ROWS] = blocks[dx, dy].T

    for dx in range(X):
        arrive(dx, 0)
    for cp in os_in:
        cp.wait_recv()
    for dy in (1, 3, 2):
        for dx in range(X):
            arrive(dx, dy)
    for cp in aa_in.values():
        if cp is not aa_in[0, 0]:
            cp.wait_send()
    for k in (2, 3, 0):
        send_orb(k)

    sib_in, p2_in, px_in = {}, {}, {}

    def weight(dx, k):
        return jnp.exp(-taus[dx][:1, :1] * energy[:, nblock(k)])

    def cols_part(k):
        for dy in range(1, Y):
            or_in[k, dy].wait_recv()
        rhs = orb_r[k].reshape(Y * ROWS, NB)
        acc = 0.0
        for dx in range(X):
            acc += jnp.dot(blocks_t[dx], rhs, preferred_element_type=F32) * weight(dx, k)
        p2[k] = acc.reshape(Z, C, SUB, NB)
        p2_sib[k] = p2[k, :, 1 - c].astype(BF16)
        sib_in[k] = go(remote(p2_sib.at[k], p2_rx.at[k], sib_s.at[k], sib_r.at[k], at(flip=True)))

    def cols_send(k):
        sib_in[k].wait_recv()
        p2_tx[k] = (p2[k, :, c] + p2_rx[k].astype(F32)).astype(BF16)
        for dz in (4, 3, 5, 2, 6, 1, 7):
            p2_in[k, dz] = go(
                remote(p2_tx.at[k, (z + dz) % Z], r2.at[k, dz], p2_s.at[k, dz], p2_r.at[k, dz], at(dz=dz))
            )

    def rows_part(k):
        rhs = orb_c[:, :, nblock(k)].reshape(COLS, NB)
        acc = 0.0
        for dx in range(X):
            acc += jnp.dot(blocks[dx].reshape(Y * ROWS, COLS), rhs, preferred_element_type=F32) * weight(dx, k)
        p1[k] = acc.astype(BF16).reshape(Y, ROWS, NB)
        if k:
            px_in[k] = go(remote(p1.at[k], r1x.at[k], px_s.at[k], px_r.at[k], at(dx=k)))

    cols_part(1)
    rows_part(1)
    cols_send(1)
    rows_part(2)
    cols_part(2)
    rows_part(3)
    cols_send(2)
    rows_part(0)
    cols_part(3)
    cols_send(3)
    cols_part(0)
    cols_send(0)

    def cols_sum(k):
        total = p2_tx[k, z].astype(F32)
        for dz in (1, 7, 2, 6, 3, 5, 4):
            p2_in[k, dz].wait_recv()
            total += r2[k, dz].astype(F32)
        f_tx[k] = total
        if k:
            return go(remote(f_tx.at[k], f_rx.at[k], f_s.at[k], f_r.at[k], at(dx=k)))

    f_in = [cols_sum(1)]
    for k in range(1, X):
        px_in[k].wait_recv()
    py_in = []
    for dy in order:
        total = p1[0, dy].astype(F32)
        for k in range(1, X):
            total += r1x[k, dy].astype(F32)
        if dy:
            p1y[dy] = total.astype(BF16)
            py_in.append(go(remote(p1y.at[dy], r1y.at[dy], py_s.at[dy], py_r.at[dy], at(dy=-dy))))
    out[...] = total
    f_in.append(cols_sum(2))
    f_in.append(cols_sum(3))
    for cp in py_in:
        cp.wait_recv()
    out[...] += r1y[1].astype(F32) + r1y[2].astype(F32) + r1y[3].astype(F32)
    for k in range(1, X):
        f_in[k - 1].wait_recv()
        out[pl.ds(pl.multiple_of(((x - k) % X) * SUB, SUB), SUB)] += f_rx[k]
    cols_sum(0)
    out[pl.ds(pl.multiple_of(x * SUB, SUB), SUB)] += f_tx[0]
    for cp in sent:
        cp.wait_send()


def per_device(chi_grad, green_unocc, orbitals, tau_points, energy):
    dma, vmem = pltpu.SemaphoreType.DMA, pltpu.VMEM
    hbm = pl.BlockSpec(memory_space=pl.ANY)
    return pl.pallas_call(
        kernel,
        out_shape=jax.ShapeDtypeStruct((ROWS, NB), F32),
        in_specs=[
            hbm, hbm, hbm,
            pl.BlockSpec(memory_space=pltpu.SMEM),
            pl.BlockSpec(memory_space=pltpu.VMEM),
        ],
        out_specs=pl.BlockSpec(memory_space=pltpu.VMEM),
        scratch_shapes=[
            vmem((Y, ROWS, SPAN), BF16), vmem((Y, ROWS, SPAN), BF16), vmem((SPAN // GROUP, ROWS, GROUP), BF16),
            vmem((Y, X, ROWS, COLS), BF16), vmem((X, Y, ROWS, COLS), BF16), vmem((X, COLS, Y * ROWS), BF16),
            vmem((X, Y, ROWS, NB), BF16), vmem((Z * C, SUB, NOCC), BF16), vmem((X, 8, 128), F32),
            vmem((X, Y, ROWS, NB), BF16), vmem((X, Y, ROWS, NB), BF16),
            vmem((Y, ROWS, NB), BF16), vmem((Y, ROWS, NB), BF16),
            vmem((X, Z, C, SUB, NB), F32), vmem((X, Z, SUB, NB), BF16), vmem((X, Z, SUB, NB), BF16),
            vmem((X, Z, SUB, NB), BF16), vmem((X, Z, SUB, NB), BF16),
            vmem((X, SUB, NB), F32), vmem((X, SUB, NB), F32),
            dma((2, Y)), dma((2 + X,)), dma((X,)), dma((X,)), dma((X, Y)), dma((X, Y)),
            dma((Z,)), dma((Z,)), dma((Z,)), dma((Z,)), dma((X, Y)), dma((X, Y)),
            dma((X,)), dma((X,)), dma((Y,)), dma((Y,)), dma((X,)), dma((X,)),
            dma((X, Z)), dma((X, Z)), dma((X,)), dma((X,)),
        ],
        compiler_params=pltpu.CompilerParams(
            collective_id=1, has_side_effects=True, vmem_limit_bytes=56 * 2**20
        ),
        cost_estimate=pl.CostEstimate(flops=4 * ROWS * NPTS * NOCC, bytes_accessed=5 * 2**20, transcendentals=X * NOCC),
        name="response_backward",
    )(chi_grad[0], green_unocc[0], orbitals, tau_points, energy.reshape(1, NOCC))


def solution(mesh):
    return jax.shard_map(
        per_device,
        mesh=mesh,
        in_specs=(P("tau", "rows", None), P("tau", "rows", None), P("rows", None), P("tau"), P()),
        out_specs=P("rows", "tau"),
        check_vma=False,
    )
```

```python
import jax
import jax.numpy as jnp
from jax import lax
from jax.experimental import pallas as pl
from jax.experimental.pallas import tpu as pltpu
from jax.sharding import PartitionSpec as P

MESH = pl.DeviceIdType.MESH
BF16, F32 = jnp.bfloat16, jnp.float32
X, Y, Z, C = 4, 4, 8, 2
ROWS = 128
SUB = ROWS // X
NPTS = ROWS * Y * Z * C
COLS = NPTS // (X * Y)
SPAN = NPTS // Y
NOCC = 1536
NB = NOCC // X
GROUP = X * ROWS


def kernel(
    chi, green, orb, tau, energy, out,
    chi_v, green_v, occ_v, sbuf, blocks, blocks_t, orb_r, orb_c, taus, levels,
    p1, r1x, p1y, r1y, p2, p2_sib, p2_rx, p2_tx, r2, f_tx, f_rx,
    load_sem, own_sem, tau_s, tau_r, or_s, or_r, oc_s, oc_r, os_s, os_r, aa_s, aa_r,
    px_s, px_r, py_s, py_r, sib_s, sib_r, p2_s, p2_r, f_s, f_r,
):
    x = lax.axis_index("tau")
    row = lax.axis_index("rows")
    y, q = row // (Z * C), row % (Z * C)
    z, c = q // C, q % C

    def at(dx=0, dy=0, dz=0, flip=False):
        core = 1 - c if flip else c
        return (((y + dy) % Y) * (Z * C) + ((z + dz) % Z) * C + core, (x + dx) % X)

    def remote(src, dst, s, r, dev):
        return pltpu.make_async_remote_copy(
            src_ref=src, dst_ref=dst, send_sem=s, recv_sem=r, device_id=dev, device_id_type=MESH
        )

    def nblock(k):
        return pl.ds(pl.multiple_of(((x + k) % X) * NB, NB), NB)

    loads = {}
    for dy in (2, 1, 3, 0):
        cols = pl.ds(pl.multiple_of(((y + dy) % Y) * SPAN, SPAN), SPAN)
        loads[dy] = [
            pltpu.make_async_copy(chi.at[:, cols], chi_v.at[dy], load_sem.at[0, dy]),
            pltpu.make_async_copy(green.at[:, cols], green_v.at[dy], load_sem.at[1, dy]),
        ]
        for cp in loads[dy]:
            cp.start()
    mine = orb.at[pl.ds(pl.multiple_of(x * SUB, SUB), SUB)]
    own = [pltpu.make_async_copy(mine, orb_c.at[q], own_sem.at[0])]
    for k in range(X):
        own.append(pltpu.make_async_copy(orb.at[:, nblock(k)], orb_r.at[k, 0], own_sem.at[2 + k]))
    own.append(pltpu.make_async_copy(energy, levels, own_sem.at[2 + X]))
    for cp in own:
        cp.start()

    barrier = pltpu.get_barrier_semaphore()
    for dx in range(X):
        for dy in range(Y):
            if dx or dy:
                pl.semaphore_signal(barrier, inc=1, device_id=at(dx, dy), device_id_type=MESH)
    for dz in range(1, Z):
        pl.semaphore_signal(barrier, inc=1, device_id=at(dz=dz), device_id_type=MESH)
    pl.semaphore_signal(barrier, inc=1, device_id=at(flip=True), device_id_type=MESH)

    dst = lax.broadcasted_iota(jnp.int32, (8, GROUP), 1)
    origin = ((dst // SUB) % X) * ROWS + (dst // ROWS) * SUB + dst % SUB
    src = lax.broadcasted_iota(jnp.int32, (GROUP, GROUP), 0)
    sort = jnp.where(src == origin[:1], 1.0, 0.0).astype(BF16)

    def make(dy):
        for cp in loads[dy]:
            cp.wait()
        groups = SPAN // GROUP
        for g in range(groups):
            cols = slice(g * GROUP, (g + 1) * GROUP)
            occ_v[g] = (chi_v[dy, :, cols].astype(F32) * green_v[dy, :, cols].astype(F32)).astype(BF16)
        packed = jnp.dot(occ_v[...].reshape(groups * ROWS, GROUP), sort, preferred_element_type=F32).astype(BF16)
        for g in range(groups):
            for k in range(X):
                sbuf[dy, k, :, g * ROWS:(g + 1) * ROWS] = packed[g * ROWS:(g + 1) * ROWS, k * ROWS:(k + 1) * ROWS]

    sent = []

    def go(cp):
        cp.start()
        sent.append(cp)
        return cp

    aa_in = {}

    def send_block(dx, dy):
        part = sbuf.at[dy, (x + dx) % X]
        if dx or dy:
            cp = remote(part, blocks.at[dx, dy], aa_s.at[dx, dy], aa_r.at[dx, dy], at(dx, dy))
        else:
            cp = pltpu.make_async_copy(part, blocks.at[0, 0], own_sem.at[1])
        cp.start()
        aa_in[dx, dy] = cp

    or_in = {}

    def send_orb(k):
        for dy in (2, 1, 3):
            or_in[k, dy] = go(
                remote(orb.at[:, nblock(k)], orb_r.at[k, dy], or_s.at[k, dy], or_r.at[k, dy], at(dy=dy))
            )

    taus[0] = jnp.full((8, 128), tau[0], F32)
    make(2)
    make(1)
    make(3)
    pl.semaphore_wait(barrier, X * Y - 1 + Z - 1 + 1)
    tau_in = [go(remote(taus.at[0], taus.at[dx], tau_s.at[dx], tau_r.at[dx], at(dx=dx))) for dx in range(1, X)]
    for dx, dy in ((0, 2), (2, 2), (0, 1), (0, 3), (1, 1), (3, 3), (1, 3), (3, 1), (1, 2), (3, 2), (2, 1), (2, 3)):
        send_block(dx, dy)
    make(0)
    for dx in (2, 1, 3, 0):
        send_block(dx, 0)
    send_orb(1)
    oc_in = {
        dz: go(remote(mine, orb_c.at[q], oc_s.at[dz], oc_r.at[dz], at(dz=dz))) for dz in (4, 3, 5, 2, 6, 1, 7)
    }
    os_in = [go(remote(mine, orb_c.at[q], os_s.at[0], os_r.at[0], at(flip=True)))]

    for cp in own:
        cp.wait()
    for dz in (1, 7, 2, 6, 3, 5, 4):
        oc_in[dz].wait_recv()
        slot = ((z - dz) % Z) * C + c
        os_in.append(go(remote(orb_c.at[slot], orb_c.at[slot], os_s.at[dz], os_r.at[dz], at(flip=True))))
    send_orb(2)
    for cp in tau_in:
        cp.wait_recv()

    def arrive(dx, dy):
        if dx or dy:
            aa_in[dx, dy].wait_recv()
        else:
            aa_in[0, 0].wait()
        blocks_t[dx, :, dy * ROWS:(dy + 1) * ROWS] = blocks[dx, dy].T

    sib_in, p2_in, px_in = {}, {}, {}

    def weight(dx, k):
        return jnp.exp(-taus[dx][:1, :1] * levels[nblock(k)].reshape(1, NB))

    def cols_part(k):
        for dy in (1, 3, 2):
            or_in[k, dy].wait_recv()
        rhs = orb_r[k].reshape(Y * ROWS, NB)
        acc = 0.0
        for dx in range(X):
            acc += jnp.dot(blocks_t[dx], rhs, preferred_element_type=F32) * weight(dx, k)
        p2[k] = acc.reshape(Z, C, SUB, NB)
        p2_sib[k] = p2[k, :, 1 - c].astype(BF16)
        sib_in[k] = go(remote(p2_sib.at[k], p2_rx.at[k], sib_s.at[k], sib_r.at[k], at(flip=True)))

    def cols_send(k):
        sib_in[k].wait_recv()
        p2_tx[k] = (p2[k, :, c] + p2_rx[k].astype(F32)).astype(BF16)
        for dz in (4, 3, 5, 2, 6, 1, 7):
            p2_in[k, dz] = go(
                remote(p2_tx.at[k, (z + dz) % Z], r2.at[k, dz], p2_s.at[k, dz], p2_r.at[k, dz], at(dz=dz))
            )

    def rows_part(k):
        rhs = orb_c[:, :, nblock(k)].reshape(COLS, NB)
        acc = 0.0
        for dx in range(X):
            acc += jnp.dot(blocks[dx].reshape(Y * ROWS, COLS), rhs, preferred_element_type=F32) * weight(dx, k)
        p1[k] = acc.astype(BF16).reshape(Y, ROWS, NB)
        if k:
            rows_send(k, 1, Y - 1)

    def rows_send(k, first, count):
        part = pl.ds(first, count)
        px_in[k, first] = go(
            remote(p1.at[k, part], r1x.at[k, part], px_s.at[k, first], px_r.at[k, first], at(dx=k))
        )

    for dx, dy in aa_in:
        arrive(dx, dy)
    for dx, dy in aa_in:
        if dx or dy:
            aa_in[dx, dy].wait_send()
    for cp in os_in:
        cp.wait_recv()
    for k in (3, 0):
        send_orb(k)

    py_in = []

    def rows_sum(dy):
        total = p1[0, dy].astype(F32)
        for k in range(1, X):
            total += r1x[k, dy].astype(F32)
        if dy:
            p1y[dy] = total.astype(BF16)
            py_in.append(go(remote(p1y.at[dy], r1y.at[dy], py_s.at[dy], py_r.at[dy], at(dy=-dy))))
        else:
            out[...] = total

    def cols_sum(k):
        total = p2_tx[k, z].astype(F32)
        for dz in (1, 7, 2, 6, 3, 5, 4):
            p2_in[k, dz].wait_recv()
            total += r2[k, dz].astype(F32)
        f_tx[k] = total
        if k:
            return go(remote(f_tx.at[k], f_rx.at[k], f_s.at[k], f_r.at[k], at(dx=k)))

    cols_part(1)
    rows_part(2)
    cols_send(1)
    rows_part(1)
    cols_part(2)
    rows_part(3)
    cols_send(2)
    cols_part(3)
    rows_part(0)
    cols_send(3)
    for k in (2, 1, 3):
        rows_send(k, 0, 1)
    cols_part(0)
    f_in = [cols_sum(1)]
    cols_send(0)
    for k in range(1, X):
        px_in[k, 1].wait_recv()
    for dy in (2, 1, 3):
        rows_sum(dy)
    f_in.append(cols_sum(2))
    f_in.append(cols_sum(3))
    for k in range(1, X):
        px_in[k, 0].wait_recv()
    rows_sum(0)
    for cp in py_in:
        cp.wait_recv()
    out[...] += r1y[1].astype(F32) + r1y[2].astype(F32) + r1y[3].astype(F32)
    for k in range(1, X):
        f_in[k - 1].wait_recv()
        out[pl.ds(pl.multiple_of(((x - k) % X) * SUB, SUB), SUB)] += f_rx[k]
    cols_sum(0)
    out[pl.ds(pl.multiple_of(x * SUB, SUB), SUB)] += f_tx[0]
    for cp in sent:
        cp.wait_send()


def per_device(chi_grad, green_unocc, orbitals, tau_points, energy):
    dma, vmem = pltpu.SemaphoreType.DMA, pltpu.VMEM
    hbm = pl.BlockSpec(memory_space=pl.ANY)
    return pl.pallas_call(
        kernel,
        out_shape=jax.ShapeDtypeStruct((ROWS, NB), F32),
        in_specs=[
            hbm, hbm, hbm,
            pl.BlockSpec(memory_space=pltpu.SMEM),
            hbm,
        ],
        out_specs=pl.BlockSpec(memory_space=pltpu.VMEM),
        scratch_shapes=[
            vmem((Y, ROWS, SPAN), BF16), vmem((Y, ROWS, SPAN), BF16), vmem((SPAN // GROUP, ROWS, GROUP), BF16),
            vmem((Y, X, ROWS, COLS), BF16), vmem((X, Y, ROWS, COLS), BF16), vmem((X, COLS, Y * ROWS), BF16),
            vmem((X, Y, ROWS, NB), BF16), vmem((Z * C, SUB, NOCC), BF16), vmem((X, 8, 128), F32),
            vmem((NOCC,), F32),
            vmem((X, Y, ROWS, NB), BF16), vmem((X, Y, ROWS, NB), BF16),
            vmem((Y, ROWS, NB), BF16), vmem((Y, ROWS, NB), BF16),
            vmem((X, Z, C, SUB, NB), F32), vmem((X, Z, SUB, NB), BF16), vmem((X, Z, SUB, NB), BF16),
            vmem((X, Z, SUB, NB), BF16), vmem((X, Z, SUB, NB), BF16),
            vmem((X, SUB, NB), F32), vmem((X, SUB, NB), F32),
            dma((2, Y)), dma((3 + X,)), dma((X,)), dma((X,)), dma((X, Y)), dma((X, Y)),
            dma((Z,)), dma((Z,)), dma((Z,)), dma((Z,)), dma((X, Y)), dma((X, Y)),
            dma((X, 2)), dma((X, 2)), dma((Y,)), dma((Y,)), dma((X,)), dma((X,)),
            dma((X, Z)), dma((X, Z)), dma((X,)), dma((X,)),
        ],
        compiler_params=pltpu.CompilerParams(
            collective_id=1, has_side_effects=True, vmem_limit_bytes=56 * 2**20
        ),
        cost_estimate=pl.CostEstimate(flops=4 * ROWS * NPTS * NOCC, bytes_accessed=5 * 2**20, transcendentals=X * NOCC),
        name="response_backward",
    )(chi_grad[0], green_unocc[0], orbitals, tau_points, energy)


def solution(mesh):
    return jax.shard_map(
        per_device,
        mesh=mesh,
        in_specs=(P("tau", "rows", None), P("tau", "rows", None), P("rows", None), P("tau"), P()),
        out_specs=P("rows", "tau"),
        check_vma=False,
    )
```

```python
import jax
import jax.numpy as jnp
from jax import lax
from jax.experimental import pallas as pl
from jax.experimental.pallas import tpu as pltpu
from jax.sharding import PartitionSpec as P

MESH = pl.DeviceIdType.MESH
BF16, F32 = jnp.bfloat16, jnp.float32
X, Y, Z, C = 4, 4, 8, 2
ROWS = 128
SUB = ROWS // X
NPTS = ROWS * Y * Z * C
COLS = NPTS // (X * Y)
SPAN = NPTS // Y
NOCC = 1536
NB = NOCC // X
GROUP = X * ROWS


def kernel(
    chi, green, orb, tau, energy, out,
    chi_v, green_v, occ_v, sbuf, blocks, blocks_t, orb_r, orb_c, taus, levels,
    p1, r1x, p1y, r1y, p2, p2_sib, p2_rx, p2_tx, r2, f_tx, f_rx,
    load_sem, own_sem, tau_s, tau_r, or_s, or_r, oc_s, oc_r, os_s, os_r, aa_s, aa_r,
    px_s, px_r, py_s, py_r, sib_s, sib_r, p2_s, p2_r, f_s, f_r,
):
    x = lax.axis_index("tau")
    row = lax.axis_index("rows")
    y, q = row // (Z * C), row % (Z * C)
    z, c = q // C, q % C

    def at(dx=0, dy=0, dz=0, flip=False):
        core = 1 - c if flip else c
        return (((y + dy) % Y) * (Z * C) + ((z + dz) % Z) * C + core, (x + dx) % X)

    def remote(src, dst, s, r, dev):
        return pltpu.make_async_remote_copy(
            src_ref=src, dst_ref=dst, send_sem=s, recv_sem=r, device_id=dev, device_id_type=MESH
        )

    def nblock(k):
        return pl.ds(pl.multiple_of(((x + k) % X) * NB, NB), NB)

    loads = {}
    for dy in (2, 1, 3, 0):
        cols = pl.ds(pl.multiple_of(((y + dy) % Y) * SPAN, SPAN), SPAN)
        loads[dy] = [
            pltpu.make_async_copy(chi.at[:, cols], chi_v.at[dy], load_sem.at[0, dy]),
            pltpu.make_async_copy(green.at[:, cols], green_v.at[dy], load_sem.at[1, dy]),
        ]
        for cp in loads[dy]:
            cp.start()
    mine = orb.at[pl.ds(pl.multiple_of(x * SUB, SUB), SUB)]
    own = [pltpu.make_async_copy(mine, orb_c.at[z, c], own_sem.at[0])]
    for k in range(X):
        own.append(pltpu.make_async_copy(orb.at[:, nblock(k)], orb_r.at[k, 0], own_sem.at[2 + k]))
    own.append(pltpu.make_async_copy(energy, levels, own_sem.at[2 + X]))
    for cp in own:
        cp.start()

    barrier = pltpu.get_barrier_semaphore()
    for dx in range(X):
        for dy in range(Y):
            if dx or dy:
                pl.semaphore_signal(barrier, inc=1, device_id=at(dx, dy), device_id_type=MESH)
    for dz in range(1, Z):
        pl.semaphore_signal(barrier, inc=1, device_id=at(dz=dz), device_id_type=MESH)
    pl.semaphore_signal(barrier, inc=1, device_id=at(flip=True), device_id_type=MESH)

    dst = lax.broadcasted_iota(jnp.int32, (8, GROUP), 1)
    origin = ((dst // SUB) % X) * ROWS + (dst // ROWS) * SUB + dst % SUB
    src = lax.broadcasted_iota(jnp.int32, (GROUP, GROUP), 0)
    sort = jnp.where(src == origin[:1], 1.0, 0.0).astype(BF16)

    def make(dy):
        for cp in loads[dy]:
            cp.wait()
        groups = SPAN // GROUP
        for g in range(groups):
            cols = slice(g * GROUP, (g + 1) * GROUP)
            occ_v[g] = (chi_v[dy, :, cols].astype(F32) * green_v[dy, :, cols].astype(F32)).astype(BF16)
        packed = jnp.dot(occ_v[...].reshape(groups * ROWS, GROUP), sort, preferred_element_type=F32).astype(BF16)
        for g in range(groups):
            for k in range(X):
                sbuf[dy, k, :, g * ROWS:(g + 1) * ROWS] = packed[g * ROWS:(g + 1) * ROWS, k * ROWS:(k + 1) * ROWS]

    def go(cp):
        cp.start()
        return cp

    def drain(ref, sem):
        pltpu.make_async_copy(ref, ref, sem).wait()

    aa_in = {}

    def send_block(dx, dy):
        part = sbuf.at[dy, (x + dx) % X]
        if dx or dy:
            cp = remote(part, blocks.at[dx, dy], aa_s.at[min(dx, 1)], aa_r.at[dx, dy], at(dx, dy))
        else:
            cp = pltpu.make_async_copy(part, blocks.at[0, 0], own_sem.at[1])
        cp.start()
        aa_in[dx, dy] = cp

    def send_orb(k):
        for dy in (2, 1, 3):
            go(remote(orb.at[:, nblock(k)], orb_r.at[k, dy], or_s, or_r.at[k], at(dy=dy)))

    taus[0] = jnp.full((8, 128), tau[0], F32)
    make(2)
    pl.semaphore_wait(barrier, X * Y - 1 + Z - 1 + 1)
    send_block(0, 2)
    send_block(2, 2)
    oc_in = {dz: go(remote(mine, orb_c.at[z, c], oc_s, oc_r.at[dz], at(dz=dz))) for dz in (4, 3, 5, 2, 6, 1, 7)}
    go(remote(mine, orb_c.at[z, c], os_s, os_r, at(flip=True)))
    for dx in range(1, X):
        go(remote(taus.at[0], taus.at[dx], tau_s, tau_r, at(dx=dx)))
    make(1)
    send_block(0, 1)
    send_block(1, 1)
    make(3)
    for dx, dy in ((0, 3), (3, 3), (1, 3), (3, 1), (1, 2), (3, 2), (2, 1), (2, 3)):
        send_block(dx, dy)
    make(0)
    for dx in (2, 1, 3, 0):
        send_block(dx, 0)
    send_orb(1)

    for cp in own:
        cp.wait()
    for dz in (1, 7, 2, 6, 3, 5, 4):
        oc_in[dz].wait_recv()
        slot = orb_c.at[(z - dz) % Z, c]
        go(remote(slot, slot, os_s, os_r, at(flip=True)))
    send_orb(2)
    drain(taus.at[pl.ds(1, X - 1)], tau_r)

    def arrive(dx, dy):
        if dx or dy:
            aa_in[dx, dy].wait_recv()
        else:
            aa_in[0, 0].wait()
        blocks_t[dx, :, dy * ROWS:(dy + 1) * ROWS] = blocks[dx, dy].T

    sib_in = {}

    def weight(dx, k):
        return jnp.exp(-taus[dx][:1, :1] * levels[nblock(k)].reshape(1, NB))

    def cols_part(k):
        drain(orb_r.at[k, pl.ds(1, Y - 1)], or_r.at[k])
        rhs = orb_r[k].reshape(Y * ROWS, NB)
        acc = 0.0
        for dx in range(X):
            acc += jnp.dot(blocks_t[dx], rhs, preferred_element_type=F32) * weight(dx, k)
        p2[k] = acc.reshape(Z, C, SUB, NB)
        p2_sib[k] = p2[k, :, 1 - c].astype(BF16)
        sib_in[k] = go(remote(p2_sib.at[k], p2_rx.at[k], sib_s, sib_r.at[k], at(flip=True)))

    def cols_send(k):
        sib_in[k].wait_recv()
        p2_tx[k] = (p2[k, :, c] + p2_rx[k].astype(F32)).astype(BF16)
        for dz in (4, 3, 5, 2, 6, 1, 7):
            go(remote(p2_tx.at[k, (z + dz) % Z], r2.at[k, dz], p2_s, p2_r.at[k], at(dz=dz)))

    def rows_part(k):
        rhs = orb_c[:, :, :, nblock(k)].reshape(COLS, NB)
        acc = 0.0
        for dx in range(X):
            acc += jnp.dot(blocks[dx].reshape(Y * ROWS, COLS), rhs, preferred_element_type=F32) * weight(dx, k)
        p1[k] = acc.astype(BF16).reshape(Y, ROWS, NB)
        if k:
            rows_send(k, 1, Y - 1)

    def rows_send(k, first, count):
        part = pl.ds(first, count)
        go(remote(p1.at[k, part], r1x.at[k, part], px_s.at[first], px_r.at[first], at(dx=k)))

    for dx, dy in aa_in:
        arrive(dx, dy)
    drain(orb_c.at[:, 1 - c], os_r)
    for k in (3, 0):
        send_orb(k)

    def rows_sum(dy):
        total = p1[0, dy].astype(F32)
        for k in range(1, X):
            total += r1x[k, dy].astype(F32)
        if dy:
            p1y[dy] = total.astype(BF16)
            go(remote(p1y.at[dy], r1y.at[dy], py_s, py_r, at(dy=-dy)))
        else:
            out[...] = total

    def cols_sum(k):
        total = p2_tx[k, z].astype(F32)
        drain(r2.at[k, pl.ds(1, Z - 1)], p2_r.at[k])
        for dz in range(1, Z):
            total += r2[k, dz].astype(F32)
        f_tx[k] = total
        if k:
            go(remote(f_tx.at[k], f_rx.at[k], f_s, f_r, at(dx=k)))

    rows_part(2)
    rows_part(1)
    cols_part(1)
    rows_part(3)
    cols_send(1)
    cols_part(2)
    cols_send(2)
    cols_part(3)
    rows_part(0)
    cols_send(3)
    for k in (2, 1, 3):
        rows_send(k, 0, 1)
    cols_part(0)
    cols_sum(1)
    cols_send(0)
    others = pl.ds(1, X - 1)
    rest = pl.ds(1, Y - 1)
    drain(r1x.at[others, rest], px_r.at[1])
    for dy in (2, 1, 3):
        rows_sum(dy)
    cols_sum(2)
    cols_sum(3)
    drain(r1x.at[others, pl.ds(0, 1)], px_r.at[0])
    rows_sum(0)
    drain(r1y.at[rest], py_r)
    out[...] += r1y[1].astype(F32) + r1y[2].astype(F32) + r1y[3].astype(F32)
    drain(f_rx.at[others], f_r)
    for k in range(1, X):
        out[pl.ds(pl.multiple_of(((x - k) % X) * SUB, SUB), SUB)] += f_rx[k]
    cols_sum(0)
    out[pl.ds(pl.multiple_of(x * SUB, SUB), SUB)] += f_tx[0]
    drain(taus.at[others], tau_s)
    drain(orb_c.at[pl.ds(1, Z - 1), 0], oc_s)
    drain(orb_c.at[:, 0], os_s)
    drain(blocks.at[0, rest], aa_s.at[0])
    drain(blocks.at[others], aa_s.at[1])
    drain(orb_r.at[:, rest], or_s)
    drain(p2_rx, sib_s)
    drain(r2.at[:, pl.ds(1, Z - 1)], p2_s)
    drain(r1x.at[others, pl.ds(0, 1)], px_s.at[0])
    drain(r1x.at[others, rest], px_s.at[1])
    drain(r1y.at[rest], py_s)
    drain(f_rx.at[others], f_s)


def per_device(chi_grad, green_unocc, orbitals, tau_points, energy):
    dma, vmem = pltpu.SemaphoreType.DMA, pltpu.VMEM
    hbm = pl.BlockSpec(memory_space=pl.ANY)
    return pl.pallas_call(
        kernel,
        out_shape=jax.ShapeDtypeStruct((ROWS, NB), F32),
        in_specs=[
            hbm, hbm, hbm,
            pl.BlockSpec(memory_space=pltpu.SMEM),
            hbm,
        ],
        out_specs=pl.BlockSpec(memory_space=pltpu.VMEM),
        scratch_shapes=[
            vmem((Y, ROWS, SPAN), BF16), vmem((Y, ROWS, SPAN), BF16), vmem((SPAN // GROUP, ROWS, GROUP), BF16),
            vmem((Y, X, ROWS, COLS), BF16), vmem((X, Y, ROWS, COLS), BF16), vmem((X, COLS, Y * ROWS), BF16),
            vmem((X, Y, ROWS, NB), BF16), vmem((Z, C, SUB, NOCC), BF16), vmem((X, 8, 128), F32),
            vmem((NOCC,), F32),
            vmem((X, Y, ROWS, NB), BF16), vmem((X, Y, ROWS, NB), BF16),
            vmem((Y, ROWS, NB), BF16), vmem((Y, ROWS, NB), BF16),
            vmem((X, Z, C, SUB, NB), F32), vmem((X, Z, SUB, NB), BF16), vmem((X, Z, SUB, NB), BF16),
            vmem((X, Z, SUB, NB), BF16), vmem((X, Z, SUB, NB), BF16),
            vmem((X, SUB, NB), F32), vmem((X, SUB, NB), F32),
            dma((2, Y)), dma((3 + X,)), dma, dma, dma, dma((X,)), dma, dma((Z,)), dma, dma, dma((2,)), dma((X, Y)),
            dma((2,)), dma((2,)), dma, dma, dma, dma((X,)), dma, dma((X,)), dma, dma,
        ],
        compiler_params=pltpu.CompilerParams(
            collective_id=1, has_side_effects=True, vmem_limit_bytes=56 * 2**20
        ),
        cost_estimate=pl.CostEstimate(flops=4 * ROWS * NPTS * NOCC, bytes_accessed=5 * 2**20, transcendentals=X * NOCC),
        name="response_backward",
    )(chi_grad[0], green_unocc[0], orbitals, tau_points, energy)


def solution(mesh):
    return jax.shard_map(
        per_device,
        mesh=mesh,
        in_specs=(P("tau", "rows", None), P("tau", "rows", None), P("rows", None), P("tau"), P()),
        out_specs=P("rows", "tau"),
        check_vma=False,
    )
```

```python
import jax
import jax.numpy as jnp
from jax import lax
from jax.experimental import pallas as pl
from jax.experimental.pallas import tpu as pltpu
from jax.sharding import PartitionSpec as P

MESH = pl.DeviceIdType.MESH
BF16, F32 = jnp.bfloat16, jnp.float32
X, Y, Z, C = 4, 4, 8, 2
ROWS = 128
SUB = ROWS // X
NPTS = ROWS * Y * Z * C
COLS = NPTS // (X * Y)
SPAN = NPTS // Y
NOCC = 1536
NB = NOCC // X
GROUP = X * ROWS


def kernel(
    chi, green, orb, tau, energy, out,
    chi_v, green_v, occ_v, sbuf, blocks, blocks_t, orb_r, orb_c, taus, levels,
    p1, r1x, p1y, r1y, p2, p2_sib, p2_rx, p2_tx, r2, f_tx, f_rx,
    load_sem, own_sem, tau_s, tau_r, or_s, or_r, oc_s, oc_r, os_s, os_r, aa_s, aa_r,
    px_s, px_r, py_s, py_r, sib_s, sib_r, p2_s, p2_r, f_s, f_r,
):
    x = lax.axis_index("tau")
    row = lax.axis_index("rows")
    y, q = row // (Z * C), row % (Z * C)
    z, c = q // C, q % C

    def at(dx=0, dy=0, dz=0, flip=False):
        core = 1 - c if flip else c
        return (((y + dy) % Y) * (Z * C) + ((z + dz) % Z) * C + core, (x + dx) % X)

    def remote(src, dst, s, r, dev):
        return pltpu.make_async_remote_copy(
            src_ref=src, dst_ref=dst, send_sem=s, recv_sem=r, device_id=dev, device_id_type=MESH
        )

    def nblock(k):
        return pl.ds(pl.multiple_of(((x + k) % X) * NB, NB), NB)

    loads = {}
    for dy in (2, 1, 3, 0):
        cols = pl.ds(pl.multiple_of(((y + dy) % Y) * SPAN, SPAN), SPAN)
        loads[dy] = [
            pltpu.make_async_copy(chi.at[:, cols], chi_v.at[dy], load_sem.at[0, dy]),
            pltpu.make_async_copy(green.at[:, cols], green_v.at[dy], load_sem.at[1, dy]),
        ]
        for cp in loads[dy]:
            cp.start()
    mine = orb.at[pl.ds(pl.multiple_of(x * SUB, SUB), SUB)]
    own = [pltpu.make_async_copy(mine, orb_c.at[z, c], own_sem.at[0])]
    for k in range(X):
        own.append(pltpu.make_async_copy(orb.at[:, nblock(k)], orb_r.at[k, 0], own_sem.at[2 + k]))
    own.append(pltpu.make_async_copy(energy, levels, own_sem.at[2 + X]))
    for cp in own:
        cp.start()

    barrier = pltpu.get_barrier_semaphore()
    for dx in range(X):
        for dy in range(Y):
            if dx or dy:
                pl.semaphore_signal(barrier, inc=1, device_id=at(dx, dy), device_id_type=MESH)
    for dz in range(1, Z):
        pl.semaphore_signal(barrier, inc=1, device_id=at(dz=dz), device_id_type=MESH)
    pl.semaphore_signal(barrier, inc=1, device_id=at(flip=True), device_id_type=MESH)

    dst = lax.broadcasted_iota(jnp.int32, (8, GROUP), 1)
    origin = ((dst // SUB) % X) * ROWS + (dst // ROWS) * SUB + dst % SUB
    src = lax.broadcasted_iota(jnp.int32, (GROUP, GROUP), 0)
    sort = jnp.where(src == origin[:1], 1.0, 0.0).astype(BF16)

    def make(dy):
        for cp in loads[dy]:
            cp.wait()
        groups = SPAN // GROUP
        for g in range(groups):
            cols = slice(g * GROUP, (g + 1) * GROUP)
            occ_v[g] = (chi_v[dy, :, cols].astype(F32) * green_v[dy, :, cols].astype(F32)).astype(BF16)
        packed = jnp.dot(occ_v[...].reshape(groups * ROWS, GROUP), sort, preferred_element_type=F32).astype(BF16)
        for g in range(groups):
            for k in range(X):
                sbuf[dy, k, :, g * ROWS:(g + 1) * ROWS] = packed[g * ROWS:(g + 1) * ROWS, k * ROWS:(k + 1) * ROWS]

    def go(cp):
        cp.start()
        return cp

    def drain(ref, sem):
        pltpu.make_async_copy(ref, ref, sem).wait()

    aa_in = {}

    def send_block(dx, dy):
        part = sbuf.at[dy, (x + dx) % X]
        if dx or dy:
            cp = remote(part, blocks.at[dx, dy], aa_s.at[min(dx, 1)], aa_r.at[dx, dy], at(dx, dy))
        else:
            cp = pltpu.make_async_copy(part, blocks.at[0, 0], own_sem.at[1])
        cp.start()
        aa_in[dx, dy] = cp

    def send_orb(k):
        for dy in (2, 1, 3):
            go(remote(orb.at[:, nblock(k)], orb_r.at[k, dy], or_s, or_r.at[k], at(dy=dy)))

    taus[0] = jnp.full((8, 128), tau[0], F32)
    make(2)
    pl.semaphore_wait(barrier, X * Y - 1 + Z - 1 + 1)
    send_block(0, 2)
    send_block(2, 2)
    oc_in = {dz: go(remote(mine, orb_c.at[z, c], oc_s, oc_r.at[dz], at(dz=dz))) for dz in (4, 3, 5, 2, 6, 1, 7)}
    go(remote(mine, orb_c.at[z, c], os_s, os_r, at(flip=True)))
    for dx in range(1, X):
        go(remote(taus.at[0], taus.at[dx], tau_s, tau_r, at(dx=dx)))
    make(1)
    send_block(0, 1)
    send_block(1, 1)
    make(3)
    for dx, dy in ((0, 3), (3, 3), (1, 3), (3, 1), (1, 2), (3, 2), (2, 1), (2, 3)):
        send_block(dx, dy)
    make(0)
    for dx in (2, 1, 3, 0):
        send_block(dx, 0)
    send_orb(1)

    for cp in own:
        cp.wait()
    for dz in (1, 7, 2, 6, 3, 5, 4):
        oc_in[dz].wait_recv()
        slot = orb_c.at[(z - dz) % Z, c]
        go(remote(slot, slot, os_s, os_r, at(flip=True)))
    send_orb(2)
    drain(taus.at[pl.ds(1, X - 1)], tau_r)

    def arrive(dx, dy):
        if dx or dy:
            aa_in[dx, dy].wait_recv()
        else:
            aa_in[0, 0].wait()
        blocks_t[dx, :, dy * ROWS:(dy + 1) * ROWS] = blocks[dx, dy].T

    sib_in = {}

    def weight(dx, k):
        return jnp.exp(-taus[dx][:1, :1] * levels[nblock(k)].reshape(1, NB))

    def cols_part(k):
        drain(orb_r.at[k, pl.ds(1, Y - 1)], or_r.at[k])
        rhs = orb_r[k].reshape(Y * ROWS, NB)
        acc = 0.0
        for dx in range(X):
            acc += jnp.dot(blocks_t[dx], rhs, preferred_element_type=F32) * weight(dx, k)
        p2[k] = acc.reshape(Z, C, SUB, NB)
        p2_sib[k] = p2[k, :, 1 - c].astype(BF16)
        sib_in[k] = go(remote(p2_sib.at[k], p2_rx.at[k], sib_s, sib_r.at[k], at(flip=True)))

    def cols_send(k):
        sib_in[k].wait_recv()
        p2_tx[k] = (p2[k, :, c] + p2_rx[k].astype(F32)).astype(BF16)
        for dz in (4, 3, 5, 2, 6, 1, 7):
            go(remote(p2_tx.at[k, (z + dz) % Z], r2.at[k, dz], p2_s, p2_r.at[k], at(dz=dz)))

    def rows_part(k):
        rhs = orb_c[:, :, :, nblock(k)].reshape(COLS, NB)
        acc = 0.0
        for dx in range(X):
            acc += jnp.dot(blocks[dx].reshape(Y * ROWS, COLS), rhs, preferred_element_type=F32) * weight(dx, k)
        p1[k] = acc.astype(BF16).reshape(Y, ROWS, NB)
        if k:
            rows_send(k, 1, Y - 1)

    def rows_send(k, first, count):
        part = pl.ds(first, count)
        go(remote(p1.at[k, part], r1x.at[k, part], px_s.at[first], px_r.at[first], at(dx=k)))

    for dx, dy in aa_in:
        arrive(dx, dy)
    drain(orb_c.at[:, 1 - c], os_r)
    for k in (3, 0):
        send_orb(k)

    def rows_sum(dy):
        total = p1[0, dy].astype(F32)
        for k in range(1, X):
            total += r1x[k, dy].astype(F32)
        if dy:
            p1y[dy] = total.astype(BF16)
            go(remote(p1y.at[dy], r1y.at[dy], py_s, py_r, at(dy=-dy)))
        else:
            out[...] = total

    def cols_sum(k):
        total = p2_tx[k, z].astype(F32)
        drain(r2.at[k, pl.ds(1, Z - 1)], p2_r.at[k])
        for dz in range(1, Z):
            total += r2[k, dz].astype(F32)
        f_tx[k] = total
        if k:
            go(remote(f_tx.at[k], f_rx.at[k], f_s, f_r, at(dx=k)))

    rows_part(2)
    rows_part(1)
    cols_part(1)
    rows_part(3)
    cols_send(1)
    cols_part(2)
    cols_send(2)
    cols_part(3)
    rows_part(0)
    cols_send(3)
    for k in (2, 1, 3):
        rows_send(k, 0, 1)
    cols_part(0)
    others = pl.ds(1, X - 1)
    rest = pl.ds(1, Y - 1)
    drain(r1x.at[others, rest], px_r.at[1])
    for dy in (2, 1, 3):
        rows_sum(dy)
    cols_send(0)
    cols_sum(1)
    cols_sum(2)
    cols_sum(3)
    drain(r1x.at[others, pl.ds(0, 1)], px_r.at[0])
    rows_sum(0)
    drain(r1y.at[rest], py_r)
    out[...] += r1y[1].astype(F32) + r1y[2].astype(F32) + r1y[3].astype(F32)
    drain(f_rx.at[others], f_r)
    for k in range(1, X):
        out[pl.ds(pl.multiple_of(((x - k) % X) * SUB, SUB), SUB)] += f_rx[k]
    cols_sum(0)
    out[pl.ds(pl.multiple_of(x * SUB, SUB), SUB)] += f_tx[0]
    drain(taus.at[others], tau_s)
    drain(orb_c.at[pl.ds(1, Z - 1), 0], oc_s)
    drain(orb_c.at[:, 0], os_s)
    drain(blocks.at[0, rest], aa_s.at[0])
    drain(blocks.at[others], aa_s.at[1])
    drain(orb_r.at[:, rest], or_s)
    drain(p2_rx, sib_s)
    drain(r2.at[:, pl.ds(1, Z - 1)], p2_s)
    drain(r1x.at[others, pl.ds(0, 1)], px_s.at[0])
    drain(r1x.at[others, rest], px_s.at[1])
    drain(r1y.at[rest], py_s)
    drain(f_rx.at[others], f_s)


def per_device(chi_grad, green_unocc, orbitals, tau_points, energy):
    dma, vmem = pltpu.SemaphoreType.DMA, pltpu.VMEM
    hbm = pl.BlockSpec(memory_space=pl.ANY)
    return pl.pallas_call(
        kernel,
        out_shape=pltpu.VMEM((ROWS, NB), F32),
        in_specs=[
            hbm, hbm, hbm,
            pl.BlockSpec(memory_space=pltpu.SMEM),
            hbm,
        ],
        out_specs=pl.BlockSpec(memory_space=pltpu.VMEM),
        scratch_shapes=[
            vmem((Y, ROWS, SPAN), BF16), vmem((Y, ROWS, SPAN), BF16), vmem((SPAN // GROUP, ROWS, GROUP), BF16),
            vmem((Y, X, ROWS, COLS), BF16), vmem((X, Y, ROWS, COLS), BF16), vmem((X, COLS, Y * ROWS), BF16),
            vmem((X, Y, ROWS, NB), BF16), vmem((Z, C, SUB, NOCC), BF16), vmem((X, 8, 128), F32),
            vmem((NOCC,), F32),
            vmem((X, Y, ROWS, NB), BF16), vmem((X, Y, ROWS, NB), BF16),
            vmem((Y, ROWS, NB), BF16), vmem((Y, ROWS, NB), BF16),
            vmem((X, Z, C, SUB, NB), F32), vmem((X, Z, SUB, NB), BF16), vmem((X, Z, SUB, NB), BF16),
            vmem((X, Z, SUB, NB), BF16), vmem((X, Z, SUB, NB), BF16),
            vmem((X, SUB, NB), F32), vmem((X, SUB, NB), F32),
            dma((2, Y)), dma((3 + X,)), dma, dma, dma, dma((X,)), dma, dma((Z,)), dma, dma, dma((2,)), dma((X, Y)),
            dma((2,)), dma((2,)), dma, dma, dma, dma((X,)), dma, dma((X,)), dma, dma,
        ],
        compiler_params=pltpu.CompilerParams(
            collective_id=1, has_side_effects=True, vmem_limit_bytes=56 * 2**20
        ),
        cost_estimate=pl.CostEstimate(flops=4 * ROWS * NPTS * NOCC, bytes_accessed=5 * 2**20, transcendentals=X * NOCC),
        name="response_backward",
    )(chi_grad[0], green_unocc[0], orbitals, tau_points, energy)


def solution(mesh):
    return jax.shard_map(
        per_device,
        mesh=mesh,
        in_specs=(P("tau", "rows", None), P("tau", "rows", None), P("rows", None), P("tau"), P()),
        out_specs=P("rows", "tau"),
        check_vma=False,
    )
```

```python
import jax
import jax.numpy as jnp
from jax import lax
from jax.experimental import pallas as pl
from jax.experimental.pallas import tpu as pltpu
from jax.sharding import PartitionSpec as P

MESH = pl.DeviceIdType.MESH
BF16, F32 = jnp.bfloat16, jnp.float32
X, Y, Z, C = 4, 4, 8, 2
ROWS = 128
SUB = ROWS // X
NPTS = ROWS * Y * Z * C
COLS = NPTS // (X * Y)
SPAN = NPTS // Y
NOCC = 1536
NB = NOCC // X
GROUP = X * ROWS


def kernel(
    chi, green, orb, tau, energy, out,
    chi_v, green_v, occ_v, sbuf, blocks, blocks_t, orb_r, orb_c, taus, levels,
    p1, r1x, p1y, r1y, p2, p2_sib, p2_rx, p2_tx, r2, f_tx, f_rx,
    load_sem, own_sem, tau_s, tau_r, or_s, or_r, oc_s, oc_r, os_s, os_r, aa_s, aa_r,
    px_s, px_r, py_s, py_r, sib_s, sib_r, p2_s, p2_r, f_s, f_r,
):
    x = lax.axis_index("tau")
    row = lax.axis_index("rows")
    y, q = row // (Z * C), row % (Z * C)
    z, c = q // C, q % C

    def at(dx=0, dy=0, dz=0, flip=False):
        core = 1 - c if flip else c
        return (((y + dy) % Y) * (Z * C) + ((z + dz) % Z) * C + core, (x + dx) % X)

    def remote(src, dst, s, r, dev):
        return pltpu.make_async_remote_copy(
            src_ref=src, dst_ref=dst, send_sem=s, recv_sem=r, device_id=dev, device_id_type=MESH
        )

    def nblock(k):
        return pl.ds(pl.multiple_of(((x + k) % X) * NB, NB), NB)

    loads = {}
    for dy in (2, 1, 3, 0):
        cols = pl.ds(pl.multiple_of(((y + dy) % Y) * SPAN, SPAN), SPAN)
        loads[dy] = [
            pltpu.make_async_copy(chi.at[:, cols], chi_v.at[dy], load_sem.at[0, dy]),
            pltpu.make_async_copy(green.at[:, cols], green_v.at[dy], load_sem.at[1, dy]),
        ]
        for cp in loads[dy]:
            cp.start()
    mine = orb.at[pl.ds(pl.multiple_of(x * SUB, SUB), SUB)]
    own = [pltpu.make_async_copy(mine, orb_c.at[z, c], own_sem.at[0])]
    for k in range(X):
        own.append(pltpu.make_async_copy(orb.at[:, nblock(k)], orb_r.at[k, 0], own_sem.at[2 + k]))
    own.append(pltpu.make_async_copy(energy, levels, own_sem.at[2 + X]))
    for cp in own:
        cp.start()

    barrier = pltpu.get_barrier_semaphore()
    for dx in range(X):
        for dy in range(Y):
            if dx or dy:
                pl.semaphore_signal(barrier, inc=1, device_id=at(dx, dy), device_id_type=MESH)
    for dz in range(1, Z):
        pl.semaphore_signal(barrier, inc=1, device_id=at(dz=dz), device_id_type=MESH)
    pl.semaphore_signal(barrier, inc=1, device_id=at(flip=True), device_id_type=MESH)

    dst = lax.broadcasted_iota(jnp.int32, (8, GROUP), 1)
    origin = ((dst // SUB) % X) * ROWS + (dst // ROWS) * SUB + dst % SUB
    src = lax.broadcasted_iota(jnp.int32, (GROUP, GROUP), 0)
    sort = jnp.where(src == origin[:1], 1.0, 0.0).astype(BF16)

    def make(dy):
        for cp in loads[dy]:
            cp.wait()
        groups = SPAN // GROUP
        for g in range(groups):
            cols = slice(g * GROUP, (g + 1) * GROUP)
            occ_v[g] = (chi_v[dy, :, cols].astype(F32) * green_v[dy, :, cols].astype(F32)).astype(BF16)
        packed = jnp.dot(occ_v[...].reshape(groups * ROWS, GROUP), sort, preferred_element_type=F32).astype(BF16)
        for g in range(groups):
            for k in range(X):
                sbuf[dy, k, :, g * ROWS:(g + 1) * ROWS] = packed[g * ROWS:(g + 1) * ROWS, k * ROWS:(k + 1) * ROWS]

    def go(cp):
        cp.start()
        return cp

    def drain(ref, sem):
        pltpu.make_async_copy(ref, ref, sem).wait()

    aa_in = {}

    def send_block(dx, dy):
        part = sbuf.at[dy, (x + dx) % X]
        if dx or dy:
            cp = remote(part, blocks.at[dx, dy], aa_s.at[min(dx, 1)], aa_r.at[dx, dy], at(dx, dy))
        else:
            cp = pltpu.make_async_copy(part, blocks.at[0, 0], own_sem.at[1])
        cp.start()
        aa_in[dx, dy] = cp

    def send_orb(k):
        for dy in (2, 1, 3):
            go(remote(orb.at[:, nblock(k)], orb_r.at[k, dy], or_s, or_r.at[k], at(dy=dy)))

    taus[0] = jnp.full((8, 128), tau[0], F32)
    make(2)
    pl.semaphore_wait(barrier, X * Y - 1 + Z - 1 + 1)
    send_block(0, 2)
    send_block(2, 2)
    oc_in = {dz: go(remote(mine, orb_c.at[z, c], oc_s, oc_r.at[dz], at(dz=dz))) for dz in (4, 3, 5, 2, 6, 1, 7)}
    go(remote(mine, orb_c.at[z, c], os_s, os_r, at(flip=True)))
    for dx in range(1, X):
        go(remote(taus.at[0], taus.at[dx], tau_s, tau_r, at(dx=dx)))
    make(1)
    send_block(0, 1)
    send_block(1, 1)
    make(3)
    for dx, dy in ((0, 3), (3, 3), (1, 3), (3, 1), (1, 2), (3, 2), (2, 1), (2, 3)):
        send_block(dx, dy)
    send_orb(1)
    make(0)
    for dx in (2, 1, 3, 0):
        send_block(dx, 0)

    for cp in own:
        cp.wait()
    for dz in (1, 7, 2, 6, 3, 5, 4):
        oc_in[dz].wait_recv()
        slot = orb_c.at[(z - dz) % Z, c]
        go(remote(slot, slot, os_s, os_r, at(flip=True)))
    send_orb(2)
    drain(taus.at[pl.ds(1, X - 1)], tau_r)

    def arrive(dx, dy):
        if dx or dy:
            aa_in[dx, dy].wait_recv()
        else:
            aa_in[0, 0].wait()
        blocks_t[dx, :, dy * ROWS:(dy + 1) * ROWS] = blocks[dx, dy].T

    sib_in = {}

    def weight(dx, k):
        return jnp.exp(-taus[dx][:1, :1] * levels[nblock(k)].reshape(1, NB))

    def cols_part(k):
        drain(orb_r.at[k, pl.ds(1, Y - 1)], or_r.at[k])
        rhs = orb_r[k].reshape(Y * ROWS, NB)
        acc = 0.0
        for dx in range(X):
            acc += jnp.dot(blocks_t[dx], rhs, preferred_element_type=F32) * weight(dx, k)
        p2[k] = acc.reshape(Z, C, SUB, NB)
        p2_sib[k] = p2[k, :, 1 - c].astype(BF16)
        sib_in[k] = go(remote(p2_sib.at[k], p2_rx.at[k], sib_s, sib_r.at[k], at(flip=True)))

    def cols_send(k):
        sib_in[k].wait_recv()
        p2_tx[k] = (p2[k, :, c] + p2_rx[k].astype(F32)).astype(BF16)
        for dz in (4, 3, 5, 2, 6, 1, 7):
            go(remote(p2_tx.at[k, (z + dz) % Z], r2.at[k, dz], p2_s, p2_r.at[k], at(dz=dz)))

    def rows_part(k):
        rhs = orb_c[:, :, :, nblock(k)].reshape(COLS, NB)
        acc = 0.0
        for dx in range(X):
            acc += jnp.dot(blocks[dx].reshape(Y * ROWS, COLS), rhs, preferred_element_type=F32) * weight(dx, k)
        p1[k] = acc.astype(BF16).reshape(Y, ROWS, NB)
        if k:
            rows_send(k, 1, Y - 1)

    def rows_send(k, first, count):
        part = pl.ds(first, count)
        go(remote(p1.at[k, part], r1x.at[k, part], px_s.at[first], px_r.at[first], at(dx=k)))

    for dx, dy in aa_in:
        arrive(dx, dy)
    drain(orb_c.at[:, 1 - c], os_r)
    for k in (3, 0):
        send_orb(k)

    def rows_sum(dy):
        total = p1[0, dy].astype(F32)
        for k in range(1, X):
            total += r1x[k, dy].astype(F32)
        if dy:
            p1y[dy] = total.astype(BF16)
            go(remote(p1y.at[dy], r1y.at[dy], py_s, py_r, at(dy=-dy)))
        else:
            out[...] = total

    def cols_sum(k):
        total = p2_tx[k, z].astype(F32)
        drain(r2.at[k, pl.ds(1, Z - 1)], p2_r.at[k])
        for dz in range(1, Z):
            total += r2[k, dz].astype(F32)
        f_tx[k] = total
        if k:
            go(remote(f_tx.at[k], f_rx.at[k], f_s, f_r, at(dx=k)))

    rows_part(2)
    cols_part(1)
    rows_part(1)
    cols_send(1)
    cols_part(2)
    rows_part(3)
    cols_send(2)
    cols_part(3)
    rows_part(0)
    cols_send(3)
    for k in (2, 1, 3):
        rows_send(k, 0, 1)
    cols_part(0)
    others = pl.ds(1, X - 1)
    rest = pl.ds(1, Y - 1)
    drain(r1x.at[others, rest], px_r.at[1])
    for dy in (2, 1, 3):
        rows_sum(dy)
    cols_send(0)
    cols_sum(1)
    cols_sum(2)
    cols_sum(3)
    drain(r1x.at[others, pl.ds(0, 1)], px_r.at[0])
    rows_sum(0)
    drain(r1y.at[rest], py_r)
    out[...] += r1y[1].astype(F32) + r1y[2].astype(F32) + r1y[3].astype(F32)
    drain(f_rx.at[others], f_r)
    for k in range(1, X):
        out[pl.ds(pl.multiple_of(((x - k) % X) * SUB, SUB), SUB)] += f_rx[k]
    cols_sum(0)
    out[pl.ds(pl.multiple_of(x * SUB, SUB), SUB)] += f_tx[0]
    drain(taus.at[others], tau_s)
    drain(orb_c.at[pl.ds(1, Z - 1), 0], oc_s)
    drain(orb_c.at[:, 0], os_s)
    drain(blocks.at[0, rest], aa_s.at[0])
    drain(blocks.at[others], aa_s.at[1])
    drain(orb_r.at[:, rest], or_s)
    drain(p2_rx, sib_s)
    drain(r2.at[:, pl.ds(1, Z - 1)], p2_s)
    drain(r1x.at[others, pl.ds(0, 1)], px_s.at[0])
    drain(r1x.at[others, rest], px_s.at[1])
    drain(r1y.at[rest], py_s)
    drain(f_rx.at[others], f_s)


def per_device(chi_grad, green_unocc, orbitals, tau_points, energy):
    dma, vmem = pltpu.SemaphoreType.DMA, pltpu.VMEM
    hbm = pl.BlockSpec(memory_space=pl.ANY)
    return pl.pallas_call(
        kernel,
        out_shape=pltpu.VMEM((ROWS, NB), F32),
        in_specs=[
            hbm, hbm, hbm,
            pl.BlockSpec(memory_space=pltpu.SMEM),
            hbm,
        ],
        out_specs=pl.BlockSpec(memory_space=pltpu.VMEM),
        scratch_shapes=[
            vmem((Y, ROWS, SPAN), BF16), vmem((Y, ROWS, SPAN), BF16), vmem((SPAN // GROUP, ROWS, GROUP), BF16),
            vmem((Y, X, ROWS, COLS), BF16), vmem((X, Y, ROWS, COLS), BF16), vmem((X, COLS, Y * ROWS), BF16),
            vmem((X, Y, ROWS, NB), BF16), vmem((Z, C, SUB, NOCC), BF16), vmem((X, 8, 128), F32),
            vmem((NOCC,), F32),
            vmem((X, Y, ROWS, NB), BF16), vmem((X, Y, ROWS, NB), BF16),
            vmem((Y, ROWS, NB), BF16), vmem((Y, ROWS, NB), BF16),
            vmem((X, Z, C, SUB, NB), F32), vmem((X, Z, SUB, NB), BF16), vmem((X, Z, SUB, NB), BF16),
            vmem((X, Z, SUB, NB), BF16), vmem((X, Z, SUB, NB), BF16),
            vmem((X, SUB, NB), F32), vmem((X, SUB, NB), F32),
            dma((2, Y)), dma((3 + X,)), dma, dma, dma, dma((X,)), dma, dma((Z,)), dma, dma, dma((2,)), dma((X, Y)),
            dma((2,)), dma((2,)), dma, dma, dma, dma((X,)), dma, dma((X,)), dma, dma,
        ],
        compiler_params=pltpu.CompilerParams(
            collective_id=1, has_side_effects=True, vmem_limit_bytes=56 * 2**20
        ),
        cost_estimate=pl.CostEstimate(flops=4 * ROWS * NPTS * NOCC, bytes_accessed=5 * 2**20, transcendentals=X * NOCC),
        name="response_backward",
    )(chi_grad[0], green_unocc[0], orbitals, tau_points, energy)


def solution(mesh):
    return jax.shard_map(
        per_device,
        mesh=mesh,
        in_specs=(P("tau", "rows", None), P("tau", "rows", None), P("rows", None), P("tau"), P()),
        out_specs=P("rows", "tau"),
        check_vma=False,
    )
```

```python
import jax
import jax.numpy as jnp
from jax import lax
from jax.experimental import pallas as pl
from jax.experimental.pallas import tpu as pltpu
from jax.sharding import PartitionSpec as P

MESH = pl.DeviceIdType.MESH
BF16, F32 = jnp.bfloat16, jnp.float32
X, Y, Z, C = 4, 4, 8, 2
ROWS = 128
SUB = ROWS // X
NPTS = ROWS * Y * Z * C
COLS = NPTS // (X * Y)
SPAN = NPTS // Y
NOCC = 1536
NB = NOCC // X
GROUP = X * ROWS


def kernel(
    chi, green, orb, tau, energy, out,
    chi_v, green_v, occ_v, sbuf, blocks, blocks_t, orb_r, orb_c, taus, levels, tau_v,
    p1, r1x, p1y, r1y, p2, p2_sib, p2_rx, p2_tx, r2, f_tx, f_rx,
    load_sem, own_sem, tau_s, tau_r, or_s, or_r, oc_s, oc_r, os_s, os_r, aa_s, aa_r,
    px_s, px_r, py_s, py_r, sib_s, sib_r, p2_s, p2_r, f_s, f_r,
):
    x = lax.axis_index("tau")
    row = lax.axis_index("rows")
    y, q = row // (Z * C), row % (Z * C)
    z, c = q // C, q % C

    def at(dx=0, dy=0, dz=0, flip=False):
        core = 1 - c if flip else c
        return (((y + dy) % Y) * (Z * C) + ((z + dz) % Z) * C + core, (x + dx) % X)

    def remote(src, dst, s, r, dev):
        return pltpu.make_async_remote_copy(
            src_ref=src, dst_ref=dst, send_sem=s, recv_sem=r, device_id=dev, device_id_type=MESH
        )

    def nblock(k):
        return pl.ds(pl.multiple_of(((x + k) % X) * NB, NB), NB)

    loads = {}
    for dy in (2, 1, 3, 0):
        cols = pl.ds(pl.multiple_of(((y + dy) % Y) * SPAN, SPAN), SPAN)
        loads[dy] = [
            pltpu.make_async_copy(chi.at[:, cols], chi_v.at[dy], load_sem.at[0, dy]),
            pltpu.make_async_copy(green.at[:, cols], green_v.at[dy], load_sem.at[1, dy]),
        ]
        for cp in loads[dy]:
            cp.start()
    mine = orb.at[pl.ds(pl.multiple_of(x * SUB, SUB), SUB)]
    own = [pltpu.make_async_copy(mine, orb_c.at[z, c], own_sem.at[0])]
    for k in range(X):
        own.append(pltpu.make_async_copy(orb.at[:, nblock(k)], orb_r.at[k, 0], own_sem.at[2 + k]))
    own.append(pltpu.make_async_copy(energy, levels, own_sem.at[2 + X]))
    tau_in = pltpu.make_async_copy(tau, tau_v, own_sem.at[3 + X])
    tau_in.start()
    for cp in own:
        cp.start()

    barrier = pltpu.get_barrier_semaphore()
    for dx in range(X):
        for dy in range(Y):
            if dx or dy:
                pl.semaphore_signal(barrier, inc=1, device_id=at(dx, dy), device_id_type=MESH)
    for dz in range(1, Z):
        pl.semaphore_signal(barrier, inc=1, device_id=at(dz=dz), device_id_type=MESH)
    pl.semaphore_signal(barrier, inc=1, device_id=at(flip=True), device_id_type=MESH)

    dst = lax.broadcasted_iota(jnp.int32, (8, GROUP), 1)
    origin = ((dst // SUB) % X) * ROWS + (dst // ROWS) * SUB + dst % SUB
    src = lax.broadcasted_iota(jnp.int32, (GROUP, GROUP), 0)
    sort = jnp.where(src == origin[:1], 1.0, 0.0).astype(BF16)

    def make(dy):
        for cp in loads[dy]:
            cp.wait()
        groups = SPAN // GROUP
        for g in range(groups):
            cols = slice(g * GROUP, (g + 1) * GROUP)
            occ_v[g] = (chi_v[dy, :, cols].astype(F32) * green_v[dy, :, cols].astype(F32)).astype(BF16)
        packed = jnp.dot(occ_v[...].reshape(groups * ROWS, GROUP), sort, preferred_element_type=F32).astype(BF16)
        for g in range(groups):
            for k in range(X):
                sbuf[dy, k, :, g * ROWS:(g + 1) * ROWS] = packed[g * ROWS:(g + 1) * ROWS, k * ROWS:(k + 1) * ROWS]

    def go(cp):
        cp.start()
        return cp

    def drain(ref, sem):
        pltpu.make_async_copy(ref, ref, sem).wait()

    aa_in = {}

    def send_block(dx, dy):
        part = sbuf.at[dy, (x + dx) % X]
        if dx or dy:
            cp = remote(part, blocks.at[dx, dy], aa_s.at[min(dx, 1)], aa_r.at[dx, dy], at(dx, dy))
        else:
            cp = pltpu.make_async_copy(part, blocks.at[0, 0], own_sem.at[1])
        cp.start()
        aa_in[dx, dy] = cp

    def send_orb(k):
        for dy in (2, 1, 3):
            go(remote(orb.at[:, nblock(k)], orb_r.at[k, dy], or_s, or_r.at[k], at(dy=dy)))

    make(2)
    tau_in.wait()
    taus[0] = jnp.full((8, 128), tau_v[0], F32)
    pl.semaphore_wait(barrier, X * Y - 1 + Z - 1 + 1)
    send_block(0, 2)
    send_block(2, 2)
    oc_in = {dz: go(remote(mine, orb_c.at[z, c], oc_s, oc_r.at[dz], at(dz=dz))) for dz in (4, 3, 5, 2, 6, 1, 7)}
    go(remote(mine, orb_c.at[z, c], os_s, os_r, at(flip=True)))
    for dx in range(1, X):
        go(remote(taus.at[0], taus.at[dx], tau_s, tau_r, at(dx=dx)))
    make(1)
    send_block(0, 1)
    send_block(1, 1)
    make(3)
    for dx, dy in ((0, 3), (3, 3), (1, 3), (3, 1), (1, 2), (3, 2), (2, 1), (2, 3)):
        send_block(dx, dy)
    send_orb(1)
    make(0)
    for dx in (2, 1, 3, 0):
        send_block(dx, 0)

    for cp in own:
        cp.wait()
    for dz in (1, 7, 2, 6, 3, 5, 4):
        oc_in[dz].wait_recv()
        slot = orb_c.at[(z - dz) % Z, c]
        go(remote(slot, slot, os_s, os_r, at(flip=True)))
    send_orb(2)
    drain(taus.at[pl.ds(1, X - 1)], tau_r)

    def arrive(dx, dy):
        if dx or dy:
            aa_in[dx, dy].wait_recv()
        else:
            aa_in[0, 0].wait()
        blocks_t[dx, :, dy * ROWS:(dy + 1) * ROWS] = blocks[dx, dy].T

    sib_in = {}

    def weight(dx, k):
        return jnp.exp(-taus[dx][:1, :1] * levels[nblock(k)].reshape(1, NB))

    def cols_part(k):
        drain(orb_r.at[k, pl.ds(1, Y - 1)], or_r.at[k])
        rhs = orb_r[k].reshape(Y * ROWS, NB)
        acc = 0.0
        for dx in range(X):
            acc += jnp.dot(blocks_t[dx], rhs, preferred_element_type=F32) * weight(dx, k)
        p2[k] = acc.reshape(Z, C, SUB, NB)
        p2_sib[k] = p2[k, :, 1 - c].astype(BF16)
        sib_in[k] = go(remote(p2_sib.at[k], p2_rx.at[k], sib_s, sib_r.at[k], at(flip=True)))

    def cols_send(k):
        sib_in[k].wait_recv()
        p2_tx[k] = (p2[k, :, c] + p2_rx[k].astype(F32)).astype(BF16)
        for dz in (4, 3, 5, 2, 6, 1, 7):
            go(remote(p2_tx.at[k, (z + dz) % Z], r2.at[k, dz], p2_s, p2_r.at[k], at(dz=dz)))

    def rows_part(k):
        rhs = orb_c[:, :, :, nblock(k)].reshape(COLS, NB)
        acc = 0.0
        for dx in range(X):
            acc += jnp.dot(blocks[dx].reshape(Y * ROWS, COLS), rhs, preferred_element_type=F32) * weight(dx, k)
        p1[k] = acc.astype(BF16).reshape(Y, ROWS, NB)
        if k:
            rows_send(k, 1, Y - 1)

    def rows_send(k, first, count):
        part = pl.ds(first, count)
        go(remote(p1.at[k, part], r1x.at[k, part], px_s.at[first], px_r.at[first], at(dx=k)))

    for dx, dy in aa_in:
        arrive(dx, dy)
    drain(orb_c.at[:, 1 - c], os_r)
    for k in (3, 0):
        send_orb(k)

    def rows_sum(dy):
        total = p1[0, dy].astype(F32)
        for k in range(1, X):
            total += r1x[k, dy].astype(F32)
        if dy:
            p1y[dy] = total.astype(BF16)
            go(remote(p1y.at[dy], r1y.at[dy], py_s, py_r, at(dy=-dy)))
        else:
            out[...] = total

    def cols_sum(k):
        total = p2_tx[k, z].astype(F32)
        drain(r2.at[k, pl.ds(1, Z - 1)], p2_r.at[k])
        for dz in range(1, Z):
            total += r2[k, dz].astype(F32)
        f_tx[k] = total
        if k:
            go(remote(f_tx.at[k], f_rx.at[k], f_s, f_r, at(dx=k)))

    rows_part(2)
    cols_part(1)
    rows_part(1)
    cols_send(1)
    cols_part(2)
    rows_part(3)
    cols_send(2)
    cols_part(3)
    rows_part(0)
    cols_send(3)
    for k in (2, 1, 3):
        rows_send(k, 0, 1)
    cols_part(0)
    others = pl.ds(1, X - 1)
    rest = pl.ds(1, Y - 1)
    drain(r1x.at[others, rest], px_r.at[1])
    for dy in (2, 1, 3):
        rows_sum(dy)
    cols_send(0)
    cols_sum(1)
    cols_sum(2)
    cols_sum(3)
    drain(r1x.at[others, pl.ds(0, 1)], px_r.at[0])
    rows_sum(0)
    drain(r1y.at[rest], py_r)
    out[...] += r1y[1].astype(F32) + r1y[2].astype(F32) + r1y[3].astype(F32)
    drain(f_rx.at[others], f_r)
    for k in range(1, X):
        out[pl.ds(pl.multiple_of(((x - k) % X) * SUB, SUB), SUB)] += f_rx[k]
    cols_sum(0)
    out[pl.ds(pl.multiple_of(x * SUB, SUB), SUB)] += f_tx[0]
    drain(taus.at[others], tau_s)
    drain(orb_c.at[pl.ds(1, Z - 1), 0], oc_s)
    drain(orb_c.at[:, 0], os_s)
    drain(blocks.at[0, rest], aa_s.at[0])
    drain(blocks.at[others], aa_s.at[1])
    drain(orb_r.at[:, rest], or_s)
    drain(p2_rx, sib_s)
    drain(r2.at[:, pl.ds(1, Z - 1)], p2_s)
    drain(r1x.at[others, pl.ds(0, 1)], px_s.at[0])
    drain(r1x.at[others, rest], px_s.at[1])
    drain(r1y.at[rest], py_s)
    drain(f_rx.at[others], f_s)


def per_device(chi_grad, green_unocc, orbitals, tau_points, energy):
    dma, vmem = pltpu.SemaphoreType.DMA, pltpu.VMEM
    hbm = pl.BlockSpec(memory_space=pl.ANY)
    return pl.pallas_call(
        kernel,
        out_shape=pltpu.VMEM((ROWS, NB), F32),
        in_specs=[
            hbm, hbm, hbm,
            hbm, hbm,
        ],
        out_specs=pl.BlockSpec(memory_space=pltpu.VMEM),
        scratch_shapes=[
            vmem((Y, ROWS, SPAN), BF16), vmem((Y, ROWS, SPAN), BF16), vmem((SPAN // GROUP, ROWS, GROUP), BF16),
            vmem((Y, X, ROWS, COLS), BF16), vmem((X, Y, ROWS, COLS), BF16), vmem((X, COLS, Y * ROWS), BF16),
            vmem((X, Y, ROWS, NB), BF16), vmem((Z, C, SUB, NOCC), BF16), vmem((X, 8, 128), F32),
            vmem((NOCC,), F32), pltpu.SMEM((1,), F32),
            vmem((X, Y, ROWS, NB), BF16), vmem((X, Y, ROWS, NB), BF16),
            vmem((Y, ROWS, NB), BF16), vmem((Y, ROWS, NB), BF16),
            vmem((X, Z, C, SUB, NB), F32), vmem((X, Z, SUB, NB), BF16), vmem((X, Z, SUB, NB), BF16),
            vmem((X, Z, SUB, NB), BF16), vmem((X, Z, SUB, NB), BF16),
            vmem((X, SUB, NB), F32), vmem((X, SUB, NB), F32),
            dma((2, Y)), dma((4 + X,)), dma, dma, dma, dma((X,)), dma, dma((Z,)), dma, dma, dma((2,)), dma((X, Y)),
            dma((2,)), dma((2,)), dma, dma, dma, dma((X,)), dma, dma((X,)), dma, dma,
        ],
        compiler_params=pltpu.CompilerParams(
            collective_id=1, has_side_effects=True, vmem_limit_bytes=56 * 2**20
        ),
        cost_estimate=pl.CostEstimate(flops=4 * ROWS * NPTS * NOCC, bytes_accessed=5 * 2**20, transcendentals=X * NOCC),
        name="response_backward",
    )(chi_grad[0], green_unocc[0], orbitals, tau_points, energy)


def solution(mesh):
    return jax.shard_map(
        per_device,
        mesh=mesh,
        in_specs=(P("tau", "rows", None), P("tau", "rows", None), P("rows", None), P("tau"), P()),
        out_specs=P("rows", "tau"),
        check_vma=False,
    )
```
